32 devices in a mesh: region: 4 (over y, core), row: 2 (over x), col: 4 (over z).
Axes of the slice: x: 2, y: 2, z: 4, core: 2. Of those that a mesh axis runs over, the one named last changes fastest.
Arguments:
- noisy_field: bfloat16 [4, 256, 512, 128], P('region', 'row', 'col'), may hold values from -40 to 40
- coarse_cells: float32 [8192, 640], P(('region', 'row', 'col')), may hold values from -6 to 6
- coarse_proj: float32 [640, 128], replicated, may hold values from -0.25 to 0.25
- kernel_first: bfloat16 [3, 3, 128, 128], replicated, may hold values from -0.1875 to 0.1875
- kernel_second: bfloat16 [3, 3, 128, 128], replicated, may hold values from -0.1875 to 0.1875
- gain_first: float32 [128], replicated, may hold values from 0.25 to 1.75
- shift_first: float32 [128], replicated, may hold values from -3 to 3
- gain_second: float32 [128], replicated, may hold values from 0.25 to 1.75
- shift_second: float32 [128], replicated, may hold values from -3 to 3
- request_ids: int32 [4, 2, 4, 32, 6], P('region', 'row', 'col'), may hold values from 0 to 8191, as said below
- patch_slots: int32 [4, 2, 4, 169], P('region', 'row', 'col'), may hold values from 0 to 191, as said below
- tile_offsets: int32 [4, 2, 4, 2], P('region', 'row', 'col'), may hold values from 0 to 127
Outputs:
- denoised: bfloat16 [4, 256, 512, 128], P('region', 'row', 'col')
The draws below stay inside these ranges and needn't reach their ends.
Inputs may be any that keep to these rules, and one draw needn't show every extreme that they name: request_ids[r, i, j, o, m] is a cell of owner o: o * 256 <= value < (o + 1) * 256, owner o being the device of index o over region, row, col in that order. `patch_slots`: the 169 entries of one tile are distinct; in every draw one owner has all 6 of its entries used by every tile.
All inputs are finite; a program needn't handle non-finite values.
Results may differ from the reference program's by a relative error of at most 0.0051.
Values may be sent and summed in bfloat16 or wider, within the bound.
No kernel may reach another device: no remote copies, remote signals or barrier semaphores. Data moves between devices by JAX's collectives and lax.ppermute only.
A program may use at most 64 MiB of HBM per device.

```python
import jax
import jax.numpy as jnp
from jax import lax

C = 128
GROUPS = 32
CC = 640
TILE = 128
GT_DEV = 256
MOST = 6
STEP = 9
PATCH = 13
NEED = 169
REGIONS = 4
ROW_TILES = 2
COL_TILES = 4
NY = 256
NX = 512
GCELLS = 8192
DEVICES = 32


def slot_tables(key):
    hot_owner = jax.random.randint(jax.random.fold_in(key, 7), (), 0, DEVICES)

    def one_device(device_index):
        device_key = jax.random.fold_in(key, device_index)
        subkeys = jax.random.split(device_key, 4)
        hotness = jax.random.randint(subkeys[0], (DEVICES, 1), 1, 5)
        slot_depth = jnp.arange(MOST, dtype=jnp.int32)[None, :]
        order_noise = jax.random.permutation(subkeys[1], DEVICES * MOST).astype(jnp.int32).reshape(DEVICES, MOST)
        owner_ids = jnp.arange(DEVICES, dtype=jnp.int32)[:, None]
        scores = slot_depth * hotness * (DEVICES * MOST) + order_noise
        scores = jnp.where(owner_ids == hot_owner, slot_depth - MOST, scores)
        ranked = jnp.argsort(scores.reshape(-1), stable=True).astype(jnp.int32)
        chosen = ranked[:NEED]
        shuffled = chosen[jax.random.permutation(subkeys[2], NEED)]
        local_rows = jax.random.randint(subkeys[3], (DEVICES, MOST), 0, GT_DEV)
        requests = owner_ids * GT_DEV + local_rows
        return (requests.astype(jnp.int32), shuffled.astype(jnp.int32))
    all_requests, all_slots = jax.vmap(one_device)(jnp.arange(DEVICES, dtype=jnp.int32))
    return (all_requests.reshape(REGIONS, ROW_TILES, COL_TILES, DEVICES, MOST), all_slots.reshape(REGIONS, ROW_TILES, COL_TILES, NEED))


def draw_request_ids(key, part):
    return slot_tables(key)[0]


def draw_patch_slots(key, part):
    return slot_tables(key)[1]


def draw_noisy_field(key, part):
    subkeys = jax.random.split(jax.random.fold_in(key, 11), 4)
    row_frac = jnp.arange(NY, dtype=jnp.float32) / NY
    row_scale = 0.3 * jnp.power(3.0, row_frac)[None, :, None, None] * jnp.exp(jax.random.uniform(subkeys[0], (REGIONS, NY, 1, 1), minval=0.0, maxval=jnp.log(2.0)))
    col_scale = jnp.exp(jax.random.uniform(subkeys[1], (REGIONS, 1, NX, 1), minval=0.0, maxval=jnp.log(3.3)))
    chan_scale = jnp.exp(jax.random.uniform(subkeys[2], (REGIONS, 1, 1, C), minval=-0.4, maxval=0.4))
    base_noise = jnp.clip(jax.random.normal(subkeys[3], (REGIONS, NY, NX, C)), -4.0, 4.0)
    return (base_noise * row_scale * col_scale * chan_scale).astype(jnp.bfloat16)


def set_ends(values, stream_key, smallest, high):
    shape = values.shape
    place = [jax.random.randint(jax.random.fold_in(stream_key, axis), (), 0, shape[axis]) for axis in range(len(shape))]
    values = values.at[tuple(place)].set(smallest)
    longest = shape.index(max(shape))
    place[longest] = (place[longest] + 1) % shape[longest]
    return values.at[tuple(place)].set(high)


def shard_levels(stream_key, shape, cuts, low, largest):
    def one(axis_at, parts):
        draws = jax.random.uniform(jax.random.fold_in(jax.random.fold_in(stream_key, 6), axis_at), (parts,), jnp.float32, low / len(cuts), largest / len(cuts))
        return jnp.repeat(jnp.exp(draws), shape[axis_at] // parts).reshape((-1,) + (1,) * (len(shape) - axis_at - 1))

    factor_of = one(*cuts[0])
    for cut in cuts[1:]:
        factor_of = factor_of * one(*cut)
    return factor_of


def scatter_about(stream_key, dims, deviation, most, pieces=(), kind=jnp.bfloat16):
    level = shard_levels(stream_key, dims, pieces, -0.22, 0.18) if pieces else 1.0
    array = jax.random.normal(stream_key, dims, jnp.float32) * deviation * level
    return jnp.minimum(jnp.maximum(array, -most), most).astype(kind)


def setup_inputs(seed: int = 0) -> dict:
    key_list = jax.random.split(jax.random.key(seed), 13)
    return {
        "noisy_field": draw_noisy_field(jax.random.fold_in(key_list[12], 71), 0),
        "coarse_cells": scatter_about(key_list[1], (GCELLS, CC), 1.0, 6.0, ((0, 32),), jnp.float32),
        "coarse_proj": scatter_about(key_list[2], (CC, C), CC ** -0.5, 0.25, (), jnp.float32),
        "kernel_first": scatter_about(key_list[3], (3, 3, C, C), (9 * C) ** -0.5, 0.1875),
        "kernel_second": scatter_about(key_list[4], (3, 3, C, C), (9 * C) ** -0.5, 0.1875),
        "gain_first": jnp.clip(1.0 + 0.15 * jax.random.normal(key_list[5], (C,), jnp.float32), 0.25, 1.75),
        "shift_first": scatter_about(key_list[6], (C,), 0.5, 3.0, (), jnp.float32),
        "gain_second": jnp.clip(1.0 + 0.15 * jax.random.normal(key_list[7], (C,), jnp.float32), 0.25, 1.75),
        "shift_second": scatter_about(key_list[8], (C,), 0.5, 3.0, (), jnp.float32),
        "request_ids": draw_request_ids(jax.random.fold_in(key_list[12], 71), 0),
        "patch_slots": draw_patch_slots(jax.random.fold_in(key_list[12], 71), 0),
        "tile_offsets": set_ends(jax.random.randint(key_list[11], (REGIONS, ROW_TILES, COL_TILES, 2), 0, 128), jax.random.fold_in(key_list[11], 1), 0, 127).astype(jnp.int32),
    }


precise = lax.Precision.HIGHEST

def cubic_weights(offset, points, extent):
    position = (offset.astype(jnp.float32)[..., None] + jnp.arange(points, dtype=jnp.float32) * STEP) / 128.0 + 1.0
    centres = jnp.arange(extent, dtype=jnp.float32)
    distance = jnp.abs(position[..., :, None] - centres)
    near_part = (1.5 * distance - 2.5) * distance * distance + 1.0
    far_part = ((-0.5 * distance + 2.5) * distance - 4.0) * distance + 2.0
    return jnp.where(distance < 1.0, near_part, jnp.where(distance < 2.0, far_part, 0.0))

def convolve(source, kernel):
    return lax.conv_general_dilated(source[None].astype(jnp.float32), kernel.astype(jnp.float32), (1, 1), ((1, 1), (1, 1)), dimension_numbers=('NHWC', 'HWIO', 'NHWC'), precision=precise)[0]

def apply_norm(values, totals, squares, number, gain_vec, shift_vec):
    group_width = values.shape[-1] // GROUPS
    group_mean = totals / number
    spread = squares / number - group_mean * group_mean
    inv_scale = lax.rsqrt(spread + 1e-05)
    mean_full = jnp.repeat(group_mean, group_width)
    scale_full = jnp.repeat(inv_scale, group_width)
    return jax.nn.silu((values - mean_full) * (scale_full * gain_vec) + shift_vec)

def group_norm(values, gain_vec, shift_vec):
    grouped = values.reshape(values.shape[0], values.shape[1], GROUPS, -1)
    totals = lax.optimization_barrier(jnp.sum(grouped, axis=(0, 1, 3)))
    squares = lax.optimization_barrier(jnp.sum(grouped * grouped, axis=(0, 1, 3)))
    number = values.shape[0] * values.shape[1] * (values.shape[2] // GROUPS)
    return apply_norm(values, totals, squares, number, gain_vec, shift_vec)

def reference(noisy_field, coarse_cells, coarse_proj, kernel_first, kernel_second, gain_first, shift_first, gain_second, shift_second, request_ids, patch_slots, tile_offsets):

    def one_region(inputs):
        region_field, requests, slot_list, offsets = inputs
        listed = requests.reshape(ROW_TILES, COL_TILES, DEVICES * MOST)
        cell_ids = jnp.take_along_axis(listed, slot_list, axis=2)
        gathered = coarse_cells[cell_ids]
        projected = jnp.einsum('abkd,dc->abkc', gathered, coarse_proj, precision=precise)
        projected = projected.reshape(ROW_TILES, COL_TILES, PATCH, PATCH, C)
        row_weight = cubic_weights(offsets[:, :, 0], TILE, PATCH)
        col_weight = cubic_weights(offsets[:, :, 1], TILE, PATCH)
        partial_rows = jnp.einsum('abhi,abijc->abhjc', row_weight, projected, precision=precise)
        conditioning = jnp.einsum('abwj,abhjc->abhwc', col_weight, partial_rows, precision=precise)
        conditioning = conditioning.transpose(0, 2, 1, 3, 4).reshape(NY, NX, C)
        mixed_field = (region_field.astype(jnp.float32) + conditioning).astype(jnp.bfloat16)
        first_conv = convolve(mixed_field, kernel_first)
        hidden = group_norm(first_conv, gain_first, shift_first).astype(jnp.bfloat16)
        second = convolve(hidden, kernel_second)
        result = mixed_field.astype(jnp.float32) + group_norm(second, gain_second, shift_second)
        return result.astype(jnp.bfloat16)
    return lax.map(one_region, (noisy_field, request_ids, patch_slots, tile_offsets))
```

```python
import functools

import jax
import jax.numpy as jnp
import numpy as np
from jax import lax
from jax.experimental import pallas as pl
from jax.experimental.pallas import tpu as pltpu
from jax.sharding import PartitionSpec as P

GROUPS = 32
STEP = 9
PATCH = 13
EDGE = 5
WIDE = 144
CHUNK = 12
KCOL = 80
AXES = ("region", "row", "col")
MIB = 1 << 20

bf16 = jnp.bfloat16
f32 = jnp.float32


def column_entries():
    tile, shift, cell = [np.full(KCOL, v, np.int32) for v in (-1, 0, 0)]
    for dx in range(3):
        for b in range(PATCH):
            tile[dx * PATCH + b], shift[dx * PATCH + b], cell[dx * PATCH + b] = 0, dx, b
        for b in range(EDGE):
            at = 40 + dx * EDGE + b
            tile[at], shift[at], cell[at] = 1, dx, PATCH - EDGE + b
            at = 56 + dx * EDGE + b
            tile[at], shift[at], cell[at] = 2, dx, b
    return tile, shift, cell


def patch_rows():
    tile, cell = [], []
    for cs, cells in ((0, range(PATCH)), (1, range(PATCH - EDGE, PATCH)), (2, range(EDGE))):
        for b in cells:
            for a in range(16):
                tile.append(cs)
                cell.append(a * PATCH + b if a < PATCH else -1)
    return np.array(tile, np.int32), np.array(cell, np.int32)


NROWS = (PATCH + 2 * EDGE) * 16


def cubic(distance):
    near_part = (1.5 * distance - 2.5) * distance * distance + 1.0
    far_part = ((-0.5 * distance + 2.5) * distance - 4.0) * distance + 2.0
    return jnp.where(distance < 1.0, near_part, jnp.where(distance < 2.0, far_part, 0.0))


def weight_of(offset, local, cell):
    position = (offset + local * STEP).astype(f32) / 128.0 + 1.0
    return cubic(jnp.abs(position - cell.astype(f32)))


def params(limit):
    return pltpu.CompilerParams(vmem_limit_bytes=limit * MIB)


def cost(flops, moved, special=0):
    return pl.CostEstimate(flops=int(flops), bytes_accessed=int(moved), transcendentals=int(special))


def whole():
    return pl.BlockSpec(memory_space=pltpu.VMEM)


def smem():
    return pl.BlockSpec(memory_space=pltpu.SMEM)


def answer_kernel(sizes, meta_ref, first_ref, table_ref, out_ref, rows_ref):
    regions, rows, cols, sets, depth, block = sizes
    devices = regions * rows * cols
    first = first_ref[0]

    def one(q, carry):
        j = lax.rem(q, cols)
        i = lax.rem(lax.div(q, cols), rows)
        targets = []
        for s in range(sets):
            if s == 0:
                ti = i
            elif rows == 2:
                ti = 1 - i
            else:
                ti = i + 1 if s == 1 else i - 1
            for cs in range(3):
                tj = j if cs == 0 else (j + 1 if cs == 1 else j - 1)
                ok = (ti >= 0) & (ti < rows) & (tj >= 0) & (tj < cols)
                place = q + (ti - i) * cols + (tj - j)
                targets.append(jnp.where(ok, place, devices) * block + (s * 3 + cs) * depth)
        for m in range(depth):
            at = meta_ref[q, 0, m] - first
            row = table_ref[pl.ds(at, 1), :]
            for target in targets:
                rows_ref[pl.ds(target + m, 1), :] = row
        return carry

    lax.fori_loop(0, devices, one, 0)
    out_ref[...] = (
        rows_ref[pl.ds(0, devices * block), :].astype(bf16).reshape(devices, block, -1)
    )


def answer(sizes, meta_in, first, table):
    regions, rows, cols, sets, depth, block = sizes
    devices = regions * rows * cols
    channels = table.shape[1]
    return pl.pallas_call(
        functools.partial(answer_kernel, sizes),
        grid=(1,),
        out_shape=jax.ShapeDtypeStruct((devices, block, channels), bf16),
        in_specs=[
            pl.BlockSpec((devices, 1, 128), lambda n: (0, 0, 0), memory_space=pltpu.SMEM),
            smem(),
            whole(),
        ],
        out_specs=whole(),
        scratch_shapes=[pltpu.VMEM(((devices + 1) * block, channels), f32)],
        compiler_params=params(32),
        name="answer_rows",
    )(meta_in, first, table)


def put_shifted(x3_ref, at, values):
    x3_ref[at, :, 0:128] = pltpu.roll(values, 1, 0).astype(bf16)
    x3_ref[at, :, 128:256] = values.astype(bf16)
    x3_ref[at, :, 256:384] = pltpu.roll(values, WIDE - 1, 0).astype(bf16)


def convolve_chunk(x3_ref, kernel_ref, start, width):
    blocks = []
    for p in range(CHUNK // 2):
        blocks.append(
            jnp.concatenate([x3_ref[start + 2 * p + r, 0:width, :] for r in range(4)], axis=1)
        )
    lhs = jnp.concatenate(blocks, axis=0)
    return jnp.dot(lhs, kernel_ref[...], preferred_element_type=f32)


def noisy_conv_kernel(noisy_ref, up_ref, down_ref, side_ref, kernel_ref, out_ref, x3_ref):
    c = pl.program_id(0)
    last = pl.num_programs(0) - 1
    height = noisy_ref.shape[0]
    for i in range(CHUNK):
        f = c * CHUNK + i
        row = noisy_ref[jnp.clip(f - 2, 0, height - 1)].astype(f32)
        if i < 2:
            row = jnp.where(c == 0, up_ref[i].astype(f32), row)
        if i >= CHUNK - 2:
            row = jnp.where(c == last, down_ref[i - CHUNK + 2].astype(f32), row)
        values = jnp.concatenate([row, side_ref[i].astype(f32)], axis=0)
        put_shifted(x3_ref, f + 2, values)

    @pl.when(c == 0)
    def _():
        x3_ref[0:2] = jnp.zeros((2, WIDE, 384), bf16)

    result = convolve_chunk(x3_ref, kernel_ref, c * CHUNK, WIDE)
    for p in range(CHUNK // 2):
        for half in range(2):
            out_ref[2 * p + half] = result[
                p * WIDE : (p + 1) * WIDE, half * 128 : half * 128 + 128
            ].astype(bf16)


def noisy_conv(noisy, up, down, side, kernel):
    steps = side.shape[0] // CHUNK
    return pl.pallas_call(
        noisy_conv_kernel,
        grid=(steps,),
        out_shape=jax.ShapeDtypeStruct((side.shape[0], WIDE, 128), bf16),
        in_specs=[
            whole(),
            whole(),
            whole(),
            pl.BlockSpec((CHUNK, 16, 128), lambda n: (n, 0, 0)),
            whole(),
        ],
        out_specs=pl.BlockSpec((CHUNK, WIDE, 128), lambda n: (n, 0, 0)),
        scratch_shapes=[pltpu.VMEM((side.shape[0] + 2, WIDE, 384), bf16)],
        compiler_params=params(40),
        cost_estimate=cost(6.4e9, 1e7),
        name="noisy_conv",
    )(noisy, up, down, side, kernel)


def cond_conv_kernel(
    sets, rows_ref, pick_ref, row_ref, col_ref, kernel_ref, part_ref,
    out_ref, sums_ref, patch_ref, rhs_ref, lines_ref, mate_ref, total_ref,
):
    c = pl.program_id(0)
    last = pl.num_programs(0) - 1

    @pl.when(c == 0)
    def _():
        total_ref[...] = jnp.zeros_like(total_ref)
        mate_ref[...] = jnp.zeros_like(mate_ref)
        for s in range(sets):
            patch = jnp.dot(pick_ref[s], rows_ref[...], preferred_element_type=f32).astype(bf16)
            if s == 0:
                patch_ref[...] = patch[: PATCH * 16]
            rhs_ref[...] = jnp.zeros_like(rhs_ref)
            for dy in range(3):
                for dx in range(3):
                    q = jnp.dot(patch, kernel_ref[dy, dx], preferred_element_type=f32)
                    q = q.astype(bf16)
                    for n in range(PATCH + 2 * EDGE):
                        if n < PATCH:
                            k = dx * PATCH + n
                        elif n < PATCH + EDGE:
                            k = 40 + dx * EDGE + n - PATCH
                        else:
                            k = 56 + dx * EDGE + n - PATCH - EDGE
                        rhs_ref[dy * 16 : dy * 16 + 16, k * 128 : k * 128 + 128] = q[
                            n * 16 : n * 16 + 16
                        ]
            for cs, low, high in ((0, 0, 40), (1, 40, 56), (2, 56, 72)):
                if s == 0:
                    lhs = row_ref[0, cs]
                else:
                    lhs = jnp.concatenate(
                        [row_ref[s, cs, 0:16], row_ref[s, cs, WIDE - 16 : WIDE]], axis=0
                    )
                for k in range(low, high, 2):
                    part = jnp.dot(
                        lhs, rhs_ref[:, k * 128 : k * 128 + 256], preferred_element_type=f32
                    )
                    for half in range(2):
                        lanes = part[:, half * 128 : half * 128 + 128]
                        if s == 0:
                            for m in range(WIDE // 8):
                                lines_ref[
                                    pl.ds(m * 8 * KCOL + k + half, 8, stride=KCOL), :
                                ] = lanes[m * 8 : m * 8 + 8]
                        else:
                            if sets == 2 or s == 1:
                                mate_ref[0, 0, k + half, :] = lanes[2]
                                mate_ref[0, 1, k + half, :] = lanes[3]
                            if sets == 2 or s == 2:
                                mate_ref[1, 0, k + half, :] = lanes[18]
                                mate_ref[1, 1, k + half, :] = lanes[19]

        for g in range(WIDE):
            lines_ref[g * KCOL + 72 : g * KCOL + KCOL, :] = jnp.zeros((8, 128), f32)

    total = jnp.zeros((8, 128), f32)
    square = jnp.zeros((8, 128), f32)
    for p in range(CHUNK // 2):
        g = c * CHUNK + 2 * p
        rhs = jnp.concatenate(
            [
                lines_ref[pl.ds(pl.multiple_of((g + half) * KCOL, KCOL), KCOL), :].astype(bf16)
                for half in range(2)
            ],
            axis=1,
        )
        result = jnp.dot(col_ref[0], rhs, preferred_element_type=f32)
        if p == 1 or p == CHUNK // 2 - 1:
            if p == 1:
                which, s = jnp.where(c == 0, 0, 2), 1
            else:
                which, s = jnp.where(c == last, 1, 2), sets - 1
            rhs = jnp.concatenate(
                [mate_ref[which, half].astype(bf16) for half in range(2)], axis=1
            )
            result = result + jnp.dot(col_ref[s], rhs, preferred_element_type=f32)
        for half in range(2):
            i = 2 * p + half
            values = result[:, half * 128 : half * 128 + 128] + part_ref[i].astype(f32)
            out_ref[i] = values.astype(bf16)
            inner = values[0:128].reshape(16, 8, 128)
            if i < 3:
                inner = jnp.where(c == 0, 0.0, inner)
            if i == CHUNK - 1:
                inner = jnp.where(c == last, 0.0, inner)
            total = total + jnp.sum(inner, axis=0)
            square = square + jnp.sum(inner * inner, axis=0)
    total_ref[0] += total
    total_ref[1] += square

    @pl.when(c == last)
    def _():
        put_sums(sums_ref, total_ref)


def put_sums(sums_ref, total_ref):
    both = jnp.concatenate(
        [
            jnp.sum(total_ref[0], axis=0, keepdims=True),
            jnp.sum(total_ref[1], axis=0, keepdims=True),
            jnp.zeros((6, 128), f32),
        ],
        axis=0,
    )
    sums_ref[...] = jnp.broadcast_to(both[None], sums_ref.shape)


def cond_conv(sets, peers, rows_in, pick, row_weight, col_weight, kernel, part):
    steps = part.shape[0] // CHUNK
    return pl.pallas_call(
        functools.partial(cond_conv_kernel, sets),
        grid=(steps,),
        out_shape=[
            jax.ShapeDtypeStruct(part.shape, bf16),
            jax.ShapeDtypeStruct((peers, 8, 128), f32),
            jax.ShapeDtypeStruct((PATCH * 16, 128), bf16),
        ],
        in_specs=[whole()] * 5 + [pl.BlockSpec((CHUNK, WIDE, 128), lambda n: (n, 0, 0))],
        out_specs=[
            pl.BlockSpec((CHUNK, WIDE, 128), lambda n: (n, 0, 0)),
            whole(),
            whole(),
        ],
        scratch_shapes=[
            pltpu.VMEM((48, KCOL * 128), bf16),
            pltpu.VMEM((WIDE * KCOL, 128), f32),
            pltpu.VMEM((3, 2, KCOL, 128), f32),
            pltpu.VMEM((2, 8, 128), f32),
        ],
        compiler_params=params(56),
        cost_estimate=cost(2e9, 1e7),
        name="cond_conv",
    )(rows_in, pick, row_weight, col_weight, kernel, part)


def split(values):
    high = values.astype(bf16)
    return high, (values - high.astype(f32)).astype(bf16)


def mix_kernel(patch_ref, row_ref, col_ref, noisy_ref, out_ref, rhs_ref, lines_ref):
    c = pl.program_id(0)
    rows = noisy_ref.shape[0]

    @pl.when(c == 0)
    def _():
        for b in range(PATCH):
            rhs_ref[:, b * 128 : b * 128 + 128] = patch_ref[b * 16 : b * 16 + 16, :]
        rhs_ref[:, PATCH * 128 :] = jnp.zeros((16, 3 * 128), bf16)
        for b in range(0, 16, 2):
            rhs = rhs_ref[:, b * 128 : b * 128 + 256]
            part = jnp.dot(
                row_ref[...], jnp.concatenate([rhs, rhs], axis=0), preferred_element_type=f32
            )
            for half in range(2):
                for m in range(part.shape[0] // 8):
                    lines_ref[pl.ds(m * 128 + b + half, 8, stride=16), :] = part[
                        m * 8 : m * 8 + 8, half * 128 : half * 128 + 128
                    ]

    for p in range(rows // 2):
        at = (c * rows + 2 * p) * 16
        lines = jnp.concatenate(
            [lines_ref[pl.ds(pl.multiple_of(at + half * 16, 16), 16), :] for half in range(2)],
            axis=1,
        )
        high, low = split(lines)
        result = jnp.dot(
            col_ref[...], jnp.concatenate([high, low, high], axis=0), preferred_element_type=f32
        )
        for half in range(2):
            i = 2 * p + half
            out_ref[i] = (
                noisy_ref[i].astype(f32) + result[:, half * 128 : half * 128 + 128]
            ).astype(bf16)


def mix(patch, row_weight, col_weight, noisy):
    height = noisy.shape[0]
    rows = 8
    return pl.pallas_call(
        mix_kernel,
        grid=(height // rows,),
        out_shape=jax.ShapeDtypeStruct(noisy.shape, bf16),
        in_specs=[whole()] * 3 + [pl.BlockSpec((rows, 128, 128), lambda n: (n, 0, 0))],
        out_specs=pl.BlockSpec((rows, 128, 128), lambda n: (n, 0, 0)),
        scratch_shapes=[
            pltpu.VMEM((16, 16 * 128), bf16),
            pltpu.VMEM((height * 16, 128), f32),
        ],
        compiler_params=params(24),
        cost_estimate=cost(5e8, 8e6),
        name="mix",
    )(patch, row_weight, col_weight, noisy)


def scale_and_shift(number, sums_ref, gain_ref, shift_ref):
    sums = jnp.sum(sums_ref[...], axis=0)
    lane = lax.broadcasted_iota(jnp.int32, (128, 128), 0)
    other = lax.broadcasted_iota(jnp.int32, (128, 128), 1)
    width = 128 // GROUPS
    same = jnp.where(lane // width == other // width, 1.0, 0.0).astype(f32)
    grouped = jnp.dot(sums, same, precision=lax.Precision.HIGHEST, preferred_element_type=f32)
    mean = grouped[0:1] / number
    spread = grouped[1:2] / number - mean * mean
    scale = lax.rsqrt(spread + 1e-05) * gain_ref[...]
    return scale, shift_ref[...] - mean * scale


def half_silu(half):
    return half + half * jnp.tanh(half)


def hidden_conv_kernel(
    number, sums_ref, gain_ref, shift_ref, edge_ref, conv_ref, kernel_ref,
    out_ref, next_ref, x3_ref, total_ref,
):
    c = pl.program_id(0)
    last = pl.num_programs(0) - 1
    scale, shift = scale_and_shift(number, sums_ref, gain_ref, shift_ref)
    scale, shift = scale * 0.5, shift * 0.5
    place = lax.broadcasted_iota(jnp.int32, (16, 128), 0)
    side_ok = ((place == 0) & (edge_ref[3] > 0)) | ((place == 15) & (edge_ref[2] > 0))
    for i in range(CHUNK):
        g = c * CHUNK + i
        values = half_silu(conv_ref[i].astype(f32) * scale + shift)
        side = jnp.where(side_ok, values[128:WIDE], 0.0)
        values = jnp.concatenate([values[0:128], side], axis=0)
        if i == 2:
            values = jnp.where((c > 0) | (edge_ref[0] > 0), values, 0.0)
        if i == CHUNK - 1:
            values = jnp.where((c < last) | (edge_ref[1] > 0), values, 0.0)
        put_shifted(x3_ref, g + 2, values)

    @pl.when(c == 0)
    def _():
        x3_ref[0:2] = jnp.zeros((2, WIDE, 384), bf16)
        total_ref[...] = jnp.zeros_like(total_ref)

    result = convolve_chunk(x3_ref, kernel_ref, c * CHUNK, 128)
    total = jnp.zeros((8, 128), f32)
    square = jnp.zeros((8, 128), f32)
    for p in range(CHUNK // 2):
        for half in range(2):
            i = 2 * p + half
            values = result[p * 128 : (p + 1) * 128, half * 128 : half * 128 + 128]
            out_ref[jnp.maximum(c * CHUNK - 4 + i, 0)] = values.astype(bf16)
            inner = values.reshape(16, 8, 128)
            if i < 4:
                inner = jnp.where(c == 0, 0.0, inner)
            total = total + jnp.sum(inner, axis=0)
            square = square + jnp.sum(inner * inner, axis=0)
    total_ref[0] += total
    total_ref[1] += square

    @pl.when(c == last)
    def _():
        put_sums(next_ref, total_ref)


def hidden_conv(number, sums, gain, shift, edges, conv, kernel):
    steps = conv.shape[0] // CHUNK
    height = conv.shape[0] - 4
    return pl.pallas_call(
        functools.partial(hidden_conv_kernel, number),
        grid=(steps,),
        out_shape=[
            jax.ShapeDtypeStruct((height, 128, 128), bf16),
            jax.ShapeDtypeStruct(sums.shape, f32),
        ],
        in_specs=[
            whole(),
            whole(),
            whole(),
            smem(),
            pl.BlockSpec((CHUNK, WIDE, 128), lambda n: (n, 0, 0)),
            whole(),
        ],
        out_specs=[whole(), whole()],
        scratch_shapes=[
            pltpu.VMEM((conv.shape[0] + 2, WIDE, 384), bf16),
            pltpu.VMEM((2, 8, 128), f32),
        ],
        compiler_params=params(40),
        cost_estimate=cost(6.4e9, 1e7, 2.4e6),
        name="hidden_conv",
    )(sums, gain, shift, edges, conv, kernel)


def finish_kernel(number, sums_ref, gain_ref, shift_ref, second_ref, mixed_ref, out_ref):
    scale, shift = scale_and_shift(number, sums_ref, gain_ref, shift_ref)
    half = second_ref[...].astype(f32) * (scale * 0.5) + shift * 0.5
    out_ref[...] = (mixed_ref[...].astype(f32) + half_silu(half)).astype(bf16)


def finish(number, sums, gain, shift, second, mixed):
    rows = 16
    block = pl.BlockSpec((rows, 128, 128), lambda n: (n, 0, 0))
    return pl.pallas_call(
        functools.partial(finish_kernel, number),
        grid=(second.shape[0] // rows,),
        out_shape=jax.ShapeDtypeStruct(second.shape, bf16),
        in_specs=[whole(), whole(), whole(), block, block],
        out_specs=block,
        compiler_params=params(24),
        cost_estimate=cost(2e7, 1.2e7, 2e6),
        name="finish",
    )(sums, gain, shift, second, mixed)


def swap_borders(axis, to_low, to_high):
    count = lax.axis_size(axis)
    odd = lax.axis_index(axis) % 2 == 1
    even_pairs = [(i, i + 1) for i in range(0, count - 1, 2)]
    odd_pairs = [(i, i + 1) for i in range(1, count - 1, 2)]

    def both(pairs):
        return pairs + [(b, a) for a, b in pairs]

    first = lax.ppermute(jnp.where(odd, to_low, to_high), axis, both(even_pairs))
    if odd_pairs:
        second = lax.ppermute(jnp.where(odd, to_high, to_low), axis, both(odd_pairs))
    else:
        second = jnp.zeros_like(first)
    return jnp.where(odd, first, second), jnp.where(odd, second, first)


def block_kernel(kernel):
    none = jnp.zeros_like(kernel[:1])
    both = jnp.concatenate(
        [jnp.concatenate([kernel, none], 0), jnp.concatenate([none, kernel], 0)], axis=-1
    )
    return both.reshape(-1, both.shape[-1])


def body(
    noisy_field,
    coarse_cells,
    coarse_proj,
    kernel_first,
    kernel_second,
    gain_first,
    shift_first,
    gain_second,
    shift_second,
    request_ids,
    patch_slots,
    tile_offsets,
):
    regions, rows, cols = [lax.axis_size(axis) for axis in AXES]
    owners = regions * rows * cols
    depth = request_ids.shape[-1]
    need = patch_slots.shape[-1]
    held = coarse_cells.shape[0]
    channels = coarse_proj.shape[1]
    here_i, here_j = lax.axis_index("row"), lax.axis_index("col")
    me = lax.axis_index(AXES)
    noisy = noisy_field[0]
    height = noisy.shape[0]
    sets = 2 if rows == 2 else 3
    block = -(-sets * 3 * depth // 8) * 8
    sizes = (regions, rows, cols, sets, depth, block)

    own = jnp.concatenate([tile_offsets.reshape(-1), patch_slots.reshape(-1)])
    meta = jnp.concatenate(
        [
            request_ids.reshape(owners, depth),
            jnp.broadcast_to(own[None], (owners, own.shape[0])),
            jnp.zeros((owners, 256 - depth - own.shape[0]), jnp.int32),
        ],
        axis=1,
    ).reshape(owners, 1, 256)
    meta_in = lax.all_to_all(meta, AXES, split_axis=0, concat_axis=0, tiled=True)

    up, down = swap_borders("row", noisy[:2], noisy[height - 2 :])
    tall = [
        jnp.concatenate([up[:, cut], noisy[:, cut], down[:, cut]], axis=0)
        for cut in (slice(0, 2), slice(height - 2, height))
    ]
    left, right = swap_borders("col", tall[0], tall[1])
    side = jnp.concatenate(
        [right, jnp.zeros((height + 4, 12, channels), bf16), left], axis=1
    )
    table = jnp.dot(
        coarse_cells, coarse_proj, precision=lax.Precision.HIGHEST, preferred_element_type=f32
    )
    part = noisy_conv(noisy, up, down, side, block_kernel(kernel_first))

    first = (me * held).reshape(1).astype(jnp.int32)
    rows_out = answer(sizes, meta_in, first, table)
    rows_in = lax.all_to_all(rows_out, AXES, split_axis=0, concat_axis=0, tiled=True)

    if rows == 2:
        row_base = [0, jnp.where(here_i == 1, -height, height)]
        row_ok = [True, True]
        tile_i = [here_i, 1 - here_i]
    else:
        row_base = [0, -height, height]
        row_ok = [True, here_i > 0, here_i < rows - 1]
        tile_i = [here_i, here_i - 1, here_i + 1]
    col_base = [0, -height, height]
    col_ok = [True, here_j > 0, here_j < cols - 1]
    tile_j = [here_j, here_j - 1, here_j + 1]
    base = me - here_i * cols - here_j
    near = jnp.stack(
        [
            base + jnp.clip(ti, 0, rows - 1) * cols + jnp.clip(tj, 0, cols - 1)
            for ti in tile_i
            for tj in tile_j
        ]
    )
    near_meta = meta_in[:, 0, :][near].reshape(sets, 3, 256)
    offsets = near_meta[:, :, depth : depth + 2]
    slots = near_meta[:, :, depth + 2 : depth + 2 + need]

    tile_of, cell_of = patch_rows()
    wanted = slots[:, tile_of, np.maximum(cell_of, 0)]
    group = np.arange(sets)[:, None] * 3 + tile_of[None]
    index = (wanted // depth) * block + group * depth + wanted % depth
    index = jnp.where(cell_of[None] >= 0, index, -1)
    pick = (index[:, :, None] == jnp.arange(owners * block, dtype=jnp.int32)).astype(bf16)

    row_bases = jnp.stack([jnp.asarray(v, jnp.int32) for v in row_base])
    row_oks = jnp.stack([jnp.asarray(v) for v in row_ok])
    col_bases = jnp.array(col_base, jnp.int32)
    col_oks = jnp.stack([jnp.asarray(v) for v in col_ok])

    line = np.arange(WIDE)[:, None, None] - 3 + np.arange(3)[None, :, None] - 1
    local = line[None, None] - row_bases[:, None, None, None, None]
    inside = (local >= 0) & (local < height) & (np.arange(16) < PATCH)
    inside = inside & row_oks[:, None, None, None, None]
    row_weight = jnp.where(
        inside,
        weight_of(offsets[:, :, 0][:, :, None, None, None], local, jnp.arange(16)),
        0.0,
    )
    row_weight = row_weight.astype(bf16).reshape(sets, 3, WIDE, 48)

    entry_tile, entry_shift, entry_cell = column_entries()
    spot = np.arange(WIDE)
    spot = np.where(spot < WIDE - 8, spot, spot - WIDE)
    place = spot[:, None] + entry_shift[None] - 1
    pick_tile = np.maximum(entry_tile, 0)
    local = place - col_bases[pick_tile][None]
    inside = (local >= 0) & (local < height) & (entry_tile >= 0)[None] & col_oks[pick_tile][None]
    col_offsets = offsets[:, :, 1][:, pick_tile]
    col_weight = jnp.where(
        inside[None],
        weight_of(col_offsets[:, None, :], local[None], jnp.asarray(entry_cell)),
        0.0,
    ).astype(bf16)

    conv, sums, patch = cond_conv(
        sets,
        rows * cols,
        rows_in.reshape(owners * block, channels),
        pick,
        row_weight,
        col_weight,
        kernel_first,
        part,
    )
    sums = lax.all_to_all(sums, ("row", "col"), split_axis=0, concat_axis=0, tiled=True)

    own_offsets = tile_offsets.reshape(2)
    cells = jnp.arange(16)
    points = jnp.arange(height)
    weights = [
        jnp.where(
            cells < PATCH, weight_of(own_offsets[n], points[:, None], cells[None]), 0.0
        )
        for n in range(2)
    ]
    row_parts, col_parts = split(weights[0]), split(weights[1])
    mixed = mix(
        patch,
        jnp.concatenate(row_parts, axis=1),
        jnp.concatenate([col_parts[0], col_parts[0], col_parts[1]], axis=1),
        noisy,
    )

    number = height * height * rows * cols * (channels // GROUPS)
    edges = jnp.stack(
        [here_i > 0, here_i < rows - 1, here_j > 0, here_j < cols - 1]
    ).astype(jnp.int32)
    second, sums_two = hidden_conv(
        number,
        sums,
        gain_first.reshape(1, -1),
        shift_first.reshape(1, -1),
        edges,
        conv,
        block_kernel(kernel_second),
    )
    sums_two = lax.all_to_all(sums_two, ("row", "col"), split_axis=0, concat_axis=0, tiled=True)
    return finish(
        number,
        sums_two,
        gain_second.reshape(1, -1),
        shift_second.reshape(1, -1),
        second,
        mixed,
    )[None]


def solution(mesh):
    return jax.shard_map(
        body,
        mesh=mesh,
        in_specs=(
            P("region", "row", "col", None),
            P(("region", "row", "col"), None),
            P(),
            P(),
            P(),
            P(),
            P(),
            P(),
            P(),
            P("region", "row", "col", None, None),
            P("region", "row", "col", None),
            P("region", "row", "col", None),
        ),
        out_specs=P("region", "row", "col", None),
        check_vma=False,
    )
```
